512 devices in a mesh: row: 8 (over y, core), col: 16 (over z), layer: 4 (over x).
Axes of the slice: x: 4, y: 4, z: 16, core: 2. Of those that a mesh axis runs over, the one named last changes fastest.
Arguments:
- a_panel: bfloat16 [4, 8192, 4096], P('layer', 'row', 'col'), may hold values from -6 to 6
- b_panel: bfloat16 [4, 4096, 8192], P('layer', 'row', 'col'), may hold values from -0.375 to 0.375
- mask_a: int32 [4, 32, 16], P('layer', 'row', 'col'), may hold values from 0 to 1, as said below
- mask_b: int32 [4, 16, 32], P('layer', 'row', 'col'), may hold values from 0 to 1, as said below
- row_sizes: int32 [32], P('row'), may hold values from 128 to 256
- inner_sizes: int32 [4, 16], P('layer'), may hold values from 128 to 256
- col_sizes: int32 [32], P('col'), may hold values from 128 to 256
Outputs:
- product: float32 [8192, 8192], P(('row', 'layer'), 'col')
The draws below stay inside these ranges and needn't reach their ends.
Inputs may be any that keep to these rules, and one draw needn't show every extreme that they name: `mask_a`: 0 or 1; the share of ones differs from block row to block row; every block row of every group has at least one 1; in every draw at least one group is all ones, and some block rows of other groups may be all ones. `mask_b`: 0 or 1; the share of ones differs from block column to block column; every block column of every group has at least one 1; in every draw at least one group is all ones, and some block columns of other groups may be all ones.
All inputs are finite; a program needn't handle non-finite values.
Results may differ from the reference program's by a relative error of at most 0.0003.
Values may be sent and summed in bfloat16 or wider, within the bound.
No kernel may reach another device: no remote copies, remote signals or barrier semaphores. Data moves between devices by JAX's collectives and lax.ppermute only.
A program may use at most 64 MiB of HBM per device.

```python
import jax
import jax.numpy as jnp

BS = 256
KG = 4
MB = 32
NB = 32
KWB = 16


def pattern(key, groups, rows, cols):
    k_one, k_two, k_three, k_four, k_five = jax.random.split(key, 5)
    density = jax.random.randint(k_one, (groups, rows, 1), 2, 13)
    values = jax.random.randint(k_two, (groups, rows, cols), 0, 100)
    chosen = jax.random.randint(k_three, (groups, rows, 1), 0, cols)
    full_group = jax.random.randint(k_four, (), 0, groups)
    full_line = jax.random.randint(k_five, (groups, rows, 1), 0, 8) == 0
    col_index = jnp.arange(cols, dtype=jnp.int32)[None, None, :]
    group_index = jnp.arange(groups, dtype=jnp.int32)[:, None, None]
    forced = col_index == chosen
    dense = (group_index == full_group) | full_line
    return jnp.where(forced | dense | (values < density), 1, 0).astype(jnp.int32)


def block_sizes(key, count):
    k_one, k_two = jax.random.split(key)
    values = jax.random.randint(k_one, (count,), BS // 2, BS + 1)
    place = jax.random.randint(k_two, (), 0, count)
    other = (place + 1) % count
    index = jnp.arange(count, dtype=jnp.int32)
    values = jnp.where(index == place, BS, values)
    values = jnp.where(index == other, BS // 2, values)
    return values.astype(jnp.int32)


def draw_mask_a(key, part):
    key = jax.random.fold_in(key, 1)
    return pattern(key, KG, MB, KWB)


def draw_mask_b(key, part):
    key = jax.random.fold_in(key, 2)
    return jnp.swapaxes(pattern(key, KG, NB, KWB), 1, 2)


def draw_row_sizes(key, part):
    key = jax.random.fold_in(key, 3)
    return block_sizes(key, MB)


def draw_inner_sizes(key, part):
    key = jax.random.fold_in(key, 4)
    return block_sizes(key, KG * KWB).reshape(KG, KWB)


def draw_col_sizes(key, part):
    key = jax.random.fold_in(key, 5)
    return block_sizes(key, NB)


def levels(key, shape, cuts, low, top_value):
    def one(axis_at, blocks):
        steps = jax.random.uniform(jax.random.fold_in(jax.random.fold_in(key, 6), axis_at), (blocks,), jnp.float32, low / len(cuts), top_value / len(cuts))
        return jnp.repeat(jnp.exp(steps), shape[axis_at] // blocks).reshape((-1,) + (1,) * (len(shape) - axis_at - 1))

    gain = one(*cuts[0])
    for cut in cuts[1:]:
        gain = gain * one(*cut)
    return gain


def bell_draw(key, dims, spread, limit, cuts=(), kind=jnp.bfloat16):
    values = spread * jax.random.normal(key, dims, jnp.float32)
    if cuts:
        values = values * levels(key, dims, cuts, -0.22, 0.18)
    return jnp.clip(values, -limit, limit).astype(kind)


def setup_inputs(seed: int = 0) -> dict:
    key_list = jax.random.split(jax.random.key(seed), 8)
    return {
        "a_panel": bell_draw(key_list[0], (KG, MB * BS, KWB * BS), 1.0, 6.0, ((0, 4), (1, 8), (2, 16))),
        "b_panel": bell_draw(key_list[1], (KG, KWB * BS, NB * BS), BS ** -0.5, 0.375, ((0, 4), (1, 8), (2, 16))),
        "mask_a": draw_mask_a(jax.random.fold_in(key_list[7], 71), 0),
        "mask_b": draw_mask_b(jax.random.fold_in(key_list[7], 71), 0),
        "row_sizes": draw_row_sizes(jax.random.fold_in(key_list[7], 71), 0),
        "inner_sizes": draw_inner_sizes(jax.random.fold_in(key_list[7], 71), 0),
        "col_sizes": draw_col_sizes(jax.random.fold_in(key_list[7], 71), 0),
    }


def keep(mask, rsize, csize, bsize):
    offs = jnp.arange(bsize, dtype=jnp.int32)
    rows = (offs[None, :] < rsize[:, None]).astype(jnp.float32)
    cols = (offs[None, :] < csize[:, None]).astype(jnp.float32)
    mult = mask.astype(jnp.float32)[:, None, :, None] * rows[:, :, None, None] * cols[None, None, :, :]
    return mult.reshape(mask.shape[0] * bsize, mask.shape[1] * bsize).astype(jnp.bfloat16)


def reference(a_panel, b_panel, mask_a, mask_b, row_sizes, inner_sizes, col_sizes):
    total = jnp.zeros((a_panel.shape[1], b_panel.shape[2]), jnp.float32)
    for group in range(KG):
        a_eff = a_panel[group] * keep(mask_a[group], row_sizes, inner_sizes[group], BS)
        b_eff = b_panel[group] * keep(mask_b[group], inner_sizes[group], col_sizes, BS)
        total = total + jnp.dot(a_eff, b_eff, preferred_element_type=jnp.float32)
    return total
```

```python
import functools

import jax
import jax.numpy as jnp
from jax import lax
from jax.experimental import pallas as pl
from jax.experimental.pallas import tpu as pltpu
from jax.sharding import PartitionSpec as P

BS = 256
HALF = BS // 2
VMEM = pl.BlockSpec(memory_space=pltpu.VMEM)
SMEM = pl.BlockSpec(memory_space=pltpu.SMEM)
PARAMS = pltpu.CompilerParams(vmem_limit_bytes=40 * 1024 * 1024)


def below(shape, axis, size):
    return lax.broadcasted_iota(jnp.int32, shape, axis) < size


def mask_a_kernel(at_ref, mask_ref, rows_ref, inner_ref, a_ref, first_ref, second_ref):
    inner = inner_ref[0, at_ref[0]]
    for i in range(mask_ref.shape[1]):
        shape = (BS, BS)
        on = below(shape, 0, rows_ref[i] * mask_ref[0, i, 0]) & below(shape, 1, inner)
        block = jnp.where(on, a_ref[0, i * BS : (i + 1) * BS, :].astype(jnp.float32), 0.0)
        block = block.astype(jnp.bfloat16)
        first_ref[i * HALF : (i + 1) * HALF, :] = block[:HALF]
        second_ref[i * HALF : (i + 1) * HALF, :] = block[HALF:]


def mask_b_kernel(at_ref, mask_ref, inner_ref, cols_ref, b_ref, out_ref):
    blocks_k, blocks_n = mask_ref.shape[1], mask_ref.shape[2]
    for k in range(blocks_k):
        inner = inner_ref[0, at_ref[0] * blocks_k + k]
        for n in range(blocks_n):
            shape = (BS, BS)
            on = below(shape, 0, inner * mask_ref[0, k, n]) & below(shape, 1, cols_ref[n])
            place = (slice(k * BS, (k + 1) * BS), slice(n * BS, (n + 1) * BS))
            block = jnp.where(on, b_ref[(0,) + place].astype(jnp.float32), 0.0)
            out_ref[place] = block.astype(jnp.bfloat16)


def sum_kernel(first, count, blocks, place_ref, b_ref, *refs):
    a_refs, out_ref = refs[:count], refs[count]
    for step in range(count):
        k = lax.rem(place_ref[0] + place_ref[1] * (first + step) + 2 * blocks, blocks)
        term = jnp.dot(a_refs[step][...], b_ref[k], preferred_element_type=jnp.float32)
        if step == 0:
            out_ref[...] = term
        else:
            out_ref[...] += term


def last_kernel(last, blocks, place_ref, b_ref, a0_ref, a1_ref, p0_ref, p1_ref, q0_ref, q1_ref, out_ref):
    k = lax.rem(place_ref[0] + place_ref[1] * last + 2 * blocks, blocks)
    b = b_ref[k]
    for h, (a, p, q) in enumerate(((a0_ref, p0_ref, q0_ref), (a1_ref, p1_ref, q1_ref))):
        total = p[...] + q[...] + jnp.dot(a[...], b, preferred_element_type=jnp.float32)
        for owner in range(out_ref.shape[0]):
            out_ref[owner, h * HALF : (h + 1) * HALF, :] = total[owner * HALF : (owner + 1) * HALF]


def owners_kernel(in_ref, out_ref):
    out_ref[...] = jnp.sum(in_ref[...], axis=0)


def on_device(rows, cols, a_panel, b_panel, mask_a, mask_b, row_sizes, inner_sizes, col_sizes):
    z = lax.axis_index("col")
    row = lax.axis_index("row")
    way = 2 * lax.rem(row, 2) - 1
    swap = [(r, r ^ 1) for r in range(rows)]
    ring = [
        (r * cols + c, r * cols + (c + (1 if r % 2 == 0 else -1)) % cols)
        for r in range(rows)
        for c in range(cols)
    ]
    half = a_panel.shape[1] // 2
    width = b_panel.shape[2]
    stream = jax.ShapeDtypeStruct((half, BS), jnp.bfloat16)
    own = pl.pallas_call(
        mask_a_kernel,
        out_shape=(stream, stream),
        in_specs=[SMEM, SMEM, SMEM, SMEM, VMEM],
        out_specs=(VMEM, VMEM),
        compiler_params=PARAMS,
    )(z.reshape(1), mask_a, row_sizes, inner_sizes, a_panel)
    b_eff = pl.pallas_call(
        mask_b_kernel,
        out_shape=jax.ShapeDtypeStruct(b_panel.shape[1:], jnp.bfloat16),
        in_specs=[SMEM, SMEM, SMEM, SMEM, VMEM],
        out_specs=VMEM,
        compiler_params=PARAMS,
    )(row.reshape(1), mask_b, inner_sizes, col_sizes, b_panel)
    b_full = lax.all_gather(b_eff, "row", axis=0, tiled=True).reshape(cols, BS, width)

    other = [lax.ppermute(a, "row", swap) for a in own]
    held = [[a] for a in (*own, *other)]
    last = cols // 2
    for step in range(1, last + 1):
        for j in (2, 3, 0, 1):
            if step < last or j < 2:
                held[j].append(lax.ppermute(held[j][-1], ("row", "col"), ring))

    place = jnp.stack([z, way]).astype(jnp.int32)
    part = jax.ShapeDtypeStruct((half, width), jnp.float32)

    def total(first, shards):
        return pl.pallas_call(
            functools.partial(sum_kernel, first, len(shards), cols),
            out_shape=part,
            in_specs=[SMEM, VMEM] + [VMEM] * len(shards),
            out_specs=VMEM,
            compiler_params=PARAMS,
        )(place, b_full, *shards)

    theirs = [lax.ppermute(total(1, held[j][1:]), "row", swap) for j in (2, 3)]
    mine = [total(0, held[j][:last]) for j in (0, 1)]
    owners = a_panel.shape[1] // BS
    parts = pl.pallas_call(
        functools.partial(last_kernel, last, cols),
        out_shape=jax.ShapeDtypeStruct((owners, BS, width), jnp.float32),
        in_specs=[SMEM] + [VMEM] * 7,
        out_specs=VMEM,
        compiler_params=PARAMS,
    )(place, b_full, held[0][last], held[1][last], *mine, *theirs)
    parts = lax.all_to_all(parts, "layer", 0, 0)
    return pl.pallas_call(
        owners_kernel,
        out_shape=jax.ShapeDtypeStruct((BS, width), jnp.float32),
        in_specs=[VMEM],
        out_specs=VMEM,
        compiler_params=PARAMS,
    )(parts)


def solution(mesh):
    return jax.shard_map(
        functools.partial(on_device, mesh.shape["row"], mesh.shape["col"]),
        mesh=mesh,
        in_specs=(
            P("layer", "row", "col"),
            P("layer", "row", "col"),
            P("layer", "row", "col"),
            P("layer", "row", "col"),
            P("row"),
            P("layer", None),
            P("col"),
        ),
        out_specs=P(("row", "layer"), "col"),
        check_vma=False,
    )
```

```python
import functools

import jax
import jax.numpy as jnp
from jax import lax
from jax.experimental import pallas as pl
from jax.experimental.pallas import tpu as pltpu
from jax.sharding import Mesh, PartitionSpec as P

BS = 256
CORES = 2
SLOTS = 4
HBM = pl.BlockSpec(memory_space=pl.ANY)
VMEM = pl.BlockSpec(memory_space=pltpu.VMEM)
SMEM = pl.BlockSpec(memory_space=pltpu.SMEM)
PARAMS = pltpu.CompilerParams(vmem_limit_bytes=40 * 1024 * 1024)


def below(axis, size):
    return lax.broadcasted_iota(jnp.int32, (BS, BS), axis) < size


def masked(block, rows, columns):
    kept = jnp.where(below(0, rows) & below(1, columns), block.astype(jnp.float32), 0.0)
    return kept.astype(jnp.bfloat16)


def mask_kernel(at, mask_a, mask_b, row_sizes, inner_sizes, col_sizes, a_ref, b_ref, a_out, b_out):
    for k in range(mask_b.shape[1]):
        inner = inner_sizes[0, at[1] * mask_b.shape[1] + k]
        for n in range(mask_b.shape[2]):
            place = (slice(k * BS, (k + 1) * BS), slice(n * BS, (n + 1) * BS))
            b_out[place] = masked(b_ref[(0,) + place], inner * mask_b[0, k, n], col_sizes[n])
    inner = inner_sizes[0, at[0]]
    for i in range(mask_a.shape[1]):
        block = a_ref[0, i * BS : (i + 1) * BS, :]
        a_out[i] = masked(block, row_sizes[i] * mask_a[0, i, 0], inner)


def product_kernel(jobs, blocks, groups, adds, place, mine_ref, others_ref, *refs):
    sums = 1 + max(s for _, _, uses in jobs for s, _, _ in uses)
    count = 1 + max(i for _, _, uses in jobs for _, i, _ in uses)
    a_refs, starts = refs[:count], refs[count : count + adds]
    outs = refs[count + adds : count + adds + sums]
    slots, sems = refs[-2:]
    per_core = blocks // CORES

    def wanted(step):
        return lax.rem(place[0] + place[1] * step + blocks, blocks)

    def fetch(n):
        step, group, _ = jobs[n]
        k = wanted(step)
        index = group * per_core + (k // 4) * 2 + lax.rem(k, 2)
        here = lax.rem(k // 2, 2) == place[2]

        @pl.when(here)
        def _():
            pltpu.make_async_copy(mine_ref.at[index], slots.at[n % SLOTS], sems.at[n % SLOTS]).start()

        @pl.when(jnp.logical_not(here))
        def _():
            pltpu.make_async_copy(others_ref.at[index], slots.at[n % SLOTS], sems.at[n % SLOTS]).start()

    for n in range(min(SLOTS - 1, len(jobs))):
        fetch(n)
    for s in range(sums):
        mine = starts[s::sums]
        if mine:
            outs[s][...] = functools.reduce(lambda p, q: p + q, [r[...] for r in mine])
        else:
            outs[s][...] = jnp.zeros_like(outs[s])
    for n, (_, _, uses) in enumerate(jobs):
        if n + SLOTS - 1 < len(jobs):
            fetch(n + SLOTS - 1)
        slot = n % SLOTS
        pltpu.make_async_copy(mine_ref.at[0], slots.at[slot], sems.at[slot]).wait()
        for s, i, index in uses:
            outs[s][...] += jnp.dot(
                a_refs[i][index], slots[slot], preferred_element_type=jnp.float32
            )


def on_device(sizes, a_panel, b_panel, mask_a, mask_b, row_sizes, inner_sizes, col_sizes):
    cols, groups = sizes["col"], sizes["layer"]
    z, y, core = lax.axis_index("col"), lax.axis_index("y"), lax.axis_index("core")
    way = 2 * core - 1
    swap = [(0, 1), (1, 0)]
    ring = [
        (c * cols + i, c * cols + (i + (1, -1)[c]) % cols) for c in range(CORES) for i in range(cols)
    ]
    width = b_panel.shape[2]
    a_eff, b_eff = pl.pallas_call(
        mask_kernel,
        out_shape=(
            jax.ShapeDtypeStruct((groups, BS, BS), jnp.bfloat16),
            jax.ShapeDtypeStruct(b_panel.shape[1:], jnp.bfloat16),
        ),
        in_specs=[SMEM] * 6 + [VMEM] * 2,
        out_specs=(VMEM, VMEM),
        compiler_params=PARAMS,
    )(
        jnp.stack([z, y * CORES + core]),
        mask_a, mask_b, row_sizes, inner_sizes, col_sizes, a_panel, b_panel,
    )
    b_mine = lax.all_gather(b_eff, ("layer", "y"), axis=0, tiled=True).reshape(-1, BS, width)
    own = lax.all_to_all(a_eff, "layer", 0, 0)

    def after(value, earlier):
        return lax.optimization_barrier((value, earlier))[0]

    early = lax.ppermute(own[:2], "core", swap)
    late = lax.ppermute(own[2:], "core", swap)
    held = [[own[:3]], [jnp.concatenate([own[3:], early])], [late]]
    last = cols // 2
    sent = None
    b_others = None
    for step in range(1, last + 1):
        for j in range(3):
            value = held[j][-1]
            if step == last:
                if j == 2:
                    continue
                value = value[:1] if j == 1 else value
            if step > 1:
                value = after(value, sent)
            sent = value
            held[j].append(lax.ppermute(value, ("core", "col"), ring))
        if step == 6:
            b_others = lax.ppermute(after(b_mine, sent), "core", swap)

    def uses(step, which, first):
        spots = {
            "own": [(0, 0), (0, 1), (0, 2), (1, 0)],
            "other": [(1, 1), (1, 2), (2, 0), (2, 1)],
        }
        return [[(s, first + spots[w][g][0], spots[w][g][1]) for s, w in which] for g in range(groups)]

    place = jnp.stack([z, way, core]).astype(jnp.int32)
    part = jax.ShapeDtypeStruct((BS, width), jnp.float32)

    def products(steps, which, extra=()):
        arrays, jobs = [], []
        for step in steps:
            found = uses(step, which, len(arrays))
            if step == 0:
                found = [[u for u, (_, w) in zip(f, which) if w == "own"] for f in found]
            jobs += [(step, g, found[g]) for g in range(groups)]
            arrays += [h[step] for h in held if len(h) > step]
        sums = len(which)
        used = 1 + max(i for _, _, u in jobs for _, i, _ in u)
        return pl.pallas_call(
            functools.partial(product_kernel, jobs, cols, groups, len(extra)),
            out_shape=(part,) * sums,
            in_specs=[SMEM, HBM, HBM] + [VMEM] * (used + len(extra)),
            out_specs=(VMEM,) * sums,
            scratch_shapes=[
                pltpu.VMEM((SLOTS, BS, width), jnp.bfloat16),
                pltpu.SemaphoreType.DMA((SLOTS,)),
            ],
            compiler_params=PARAMS,
        )(place, b_mine, b_others, *arrays[:used], *extra)

    mine, others = products(range(0, 7), [(0, "own"), (1, "other")])
    (others,) = products([7], [(0, "other")], (others,))
    others = lax.ppermute(others, "core", swap)
    (mine,) = products([7, 8], [(0, "own")], (mine, others))
    return mine


def solution(mesh):
    rows, cols, layers = (mesh.shape[name] for name in ("row", "col", "layer"))
    devices = mesh.devices.reshape(rows // CORES, CORES, cols, layers)
    cores = Mesh(devices, ("y", "core", "col", "layer"))
    row = ("y", "core")
    return jax.shard_map(
        functools.partial(on_device, dict(cores.shape)),
        mesh=cores,
        in_specs=(
            P("layer", row, "col"),
            P("layer", row, "col"),
            P("layer", row, "col"),
            P("layer", row, "col"),
            P(row),
            P("layer", None),
            P("col"),
        ),
        out_specs=P((*row, "layer"), "col"),
        check_vma=False,
    )
```

```python
import functools

import jax
import jax.numpy as jnp
from jax import lax
from jax.experimental import pallas as pl
from jax.experimental.pallas import tpu as pltpu
from jax.sharding import Mesh, PartitionSpec as P

BS = 256
CORES = 2
ROWS = 1024
CUT = 688
SPARE = 3 * CUT - 2 * ROWS
HBM = pl.BlockSpec(memory_space=pl.ANY)
VMEM = pl.BlockSpec(memory_space=pltpu.VMEM)
PARAMS = pltpu.CompilerParams(vmem_limit_bytes=40 * 1024 * 1024)
SWAP = [(0, 1), (1, 0)]


def below(axis, size):
    return lax.broadcasted_iota(jnp.int32, (BS, BS), axis) < size


def masked(block, rows, columns):
    kept = jnp.where(below(0, rows) & below(1, columns), block.astype(jnp.float32), 0.0)
    return kept.astype(jnp.bfloat16)


def mask_kernel(*refs):
    count = 7
    a_out, b_out = refs[count : count + 2]
    slots, sems = refs[count + 2 : -1], refs[-1]
    copies = [pltpu.make_async_copy(refs[i], slots[i], sems.at[i]) for i in range(count)]
    for copy in copies:
        copy.start()
    for copy in copies:
        copy.wait()
    mask_a, mask_b, rows, inner, cols, a, b = slots
    columns = inner[0, lax.axis_index("col")]
    for i in range(ROWS // BS):
        place = slice(i * BS, (i + 1) * BS)
        a_out[place, :] = masked(a[0, place, :], rows[i] * mask_a[i], columns)
    first = (lax.axis_index("y") * CORES + lax.axis_index("core")) * mask_b.shape[1]
    for k in range(mask_b.shape[1]):
        for n in range(mask_b.shape[2]):
            place = (slice(k * BS, (k + 1) * BS), slice(n * BS, (n + 1) * BS))
            size = inner[0, first + k] * mask_b[0, k, n]
            b_out[place] = masked(b[(0,) + place], size, cols[n])


def product_kernel(steps, own, blocks, added, *refs):
    b_refs, refs = refs[:5], refs[5:]
    a_refs, refs = refs[: 2 * len(steps)], refs[2 * len(steps) :]
    adds, (out_ref, a_all, b_all, extra, sems) = refs[:added], refs[added:]
    z, y, core = lax.axis_index("col"), lax.axis_index("y"), lax.axis_index("core")
    way = 2 * core - 1
    first, count = steps[0], len(steps)

    chips, mine, theirs = 4, core, 1 - core
    parts = (
        (0, 0, y, mine), (0, 1, y, theirs),
        (1, 0, y + way, mine), (1, 1, y + way, theirs),
        (2, 0, y - way, theirs), (2, 1, y - way, mine),
        (3, 0, y + 2, mine), (4, 0, y + 2, theirs),
    )
    for i, at, chip, owner in parts:
        for half in range(2):
            k = (lax.rem(chip + chips, chips) * CORES + owner) * 2 + half
            step = lax.rem(way * (k - z) + blocks, blocks)

            @pl.when((step >= first) & (step < first + count))
            def _(ref=b_refs[i], start=(at * 2 + half) * BS, step=step):
                pltpu.make_async_copy(
                    ref.at[pl.ds(start, BS)], b_all.at[step - first], sems.at[0]
                ).start()

    for i in range(count):
        upper, lower = a_refs[2 * i], a_refs[2 * i + 1]
        lanes = pl.ds(i * BS, BS)
        if own:
            pieces = ((upper, 0, 0, CUT), (lower, 0, CUT, ROWS - CUT))
        else:
            done = 2 * CUT - ROWS
            pieces = ((upper, ROWS - CUT, 0, done), (lower, SPARE, done, ROWS - done))
        for ref, start, to, size in pieces:
            pltpu.make_async_copy(
                ref.at[pl.ds(start, size)], a_all.at[pl.ds(to, size), lanes], sems.at[1]
            ).start()
    for i, ref in enumerate(adds):
        pltpu.make_async_copy(ref, extra.at[i], sems.at[2 + i]).start()
    pltpu.make_async_copy(b_all, b_all, sems.at[0]).wait()
    pltpu.make_async_copy(a_all, a_all, sems.at[1]).wait()
    for i, ref in enumerate(adds):
        pltpu.make_async_copy(ref, extra.at[i], sems.at[2 + i]).wait()

    b = b_all[...].reshape(count * BS, b_all.shape[2])
    for tile in range(ROWS // BS):
        rows = pl.ds(tile * BS, BS)
        total = jnp.dot(a_all[rows, :], b, preferred_element_type=jnp.float32)
        for i in range(added):
            total = total + extra[i, rows, :]
        out_ref[rows, :] = total


def layers_kernel(in_hbm, out_ref, parts, sem):
    copy = pltpu.make_async_copy(in_hbm, parts, sem)
    copy.start()
    copy.wait()
    out_ref[...] = (parts[0] + parts[1]) + (parts[2] + parts[3])


def after(value, earlier):
    return lax.optimization_barrier((value, earlier))[0]


def on_device(sizes, a_panel, b_panel, mask_a, mask_b, row_sizes, inner_sizes, col_sizes):
    cols, chips = sizes["col"], sizes["y"]
    width = b_panel.shape[2]
    ring = [
        (c * cols + i, c * cols + (i + (1, -1)[c]) % cols) for c in range(CORES) for i in range(cols)
    ]
    args = (mask_a.reshape(-1), mask_b, row_sizes, inner_sizes, col_sizes, a_panel, b_panel)
    own, b_eff = pl.pallas_call(
        mask_kernel,
        out_shape=tuple(
            jax.ShapeDtypeStruct(p.shape[1:], jnp.bfloat16) for p in (a_panel, b_panel)
        ),
        in_specs=[pl.BlockSpec(memory_space=pltpu.HBM)] * len(args),
        out_specs=(VMEM, VMEM),
        scratch_shapes=[pltpu.SMEM(x.shape, x.dtype) for x in args[:5]]
        + [pltpu.VMEM(x.shape, x.dtype) for x in args[5:]]
        + [pltpu.SemaphoreType.DMA((len(args),))],
        compiler_params=pltpu.CompilerParams(vmem_limit_bytes=60 * 1024 * 1024),
    )(*args)

    last = cols // 2
    held = [[own[:CUT]], [], []]
    sent = held[0][0]
    with jax.named_scope("stream_0_step_1"):
        held[0].append(lax.ppermute(sent, ("core", "col"), ring))
    other = lax.ppermute(own, "core", SWAP)
    held[1] = [jnp.concatenate([own[CUT:], other[: 2 * CUT - ROWS]])]
    held[2] = [other[ROWS - CUT :]]
    def product(steps, own, pairs, adds=()):
        n = len(steps)
        arrays = [a for pair in pairs for a in pair]
        return pl.pallas_call(
            functools.partial(product_kernel, steps, own, cols, len(adds)),
            out_shape=jax.ShapeDtypeStruct((ROWS, width), jnp.float32),
            in_specs=[HBM] * (5 + len(arrays) + len(adds)),
            out_specs=VMEM,
            scratch_shapes=[
                pltpu.VMEM((ROWS, n * BS), jnp.bfloat16),
                pltpu.VMEM((n, BS, width), jnp.bfloat16),
                pltpu.VMEM((max(1, len(adds)), ROWS, width), jnp.float32),
                pltpu.SemaphoreType.DMA((2 + max(1, len(adds)),)),
            ],
            compiler_params=PARAMS,
            cost_estimate=pl.CostEstimate(
                flops=2 * ROWS * n * BS * width, bytes_accessed=2 * 2**20, transcendentals=0
            ),
        )(*b_all, *arrays, *adds)

    near_by = [
        (i * CORES + c, (i + (1, -1)[c]) % chips * CORES + c) for i in range(chips) for c in range(CORES)
    ]
    far_away = [(i, (i + 2) % chips) for i in range(chips)]
    b_all = [None] * 5
    b_other = None
    for step in range(1, last + 1):
        for j in range(3):
            if (step, j) == (1, 0) or (step, j) == (last, 2):
                continue
            value = held[j][-1]
            if (step, j) == (last, 1):
                value = value[: ROWS - CUT]
            sent = after(value, sent)
            with jax.named_scope(f"stream_{j}_step_{step}"):
                held[j].append(lax.ppermute(sent, ("core", "col"), ring))
            if (step, j) == (1, 2):
                b_other = lax.ppermute(after(b_eff, sent), "core", SWAP)
            if (step, j) == (2, 0):
                b_all[3] = lax.ppermute(after(b_eff, sent), "y", far_away)
            if (step, j) == (3, 2):
                b_all[0] = jnp.concatenate([b_eff, after(b_other, sent)])
                b_all[1] = lax.ppermute(b_all[0], ("y", "core"), near_by)
            if (step, j) == (6, 0):
                b_all[4] = lax.ppermute(after(b_all[3], sent), "core", SWAP)
            if (step, j) == (6, 1):
                b_all[2] = lax.ppermute(after(b_all[1], sent), "core", SWAP)

    steps = range(1, last)
    pairs = [(held[1][s], held[2][s]) for s in steps]
    pairs[-1] = after(pairs[-1], held[0][last - 1])
    others = lax.ppermute(product(steps, False, pairs), "core", SWAP)
    steps = range(last)
    mine = product(steps, True, [(held[0][s], held[1][s]) for s in steps])
    parts = product((last,), True, [(held[0][last], held[1][last])], (mine, others))
    parts = parts.reshape(-1, BS, width)
    parts = lax.all_to_all(parts, "layer", 0, 0)
    return pl.pallas_call(
        layers_kernel,
        out_shape=jax.ShapeDtypeStruct((BS, width), jnp.float32),
        in_specs=[HBM],
        out_specs=VMEM,
        scratch_shapes=[pltpu.VMEM(parts.shape, jnp.float32), pltpu.SemaphoreType.DMA],
        compiler_params=PARAMS,
    )(parts)


def solution(mesh):
    rows, cols, layers = (mesh.shape[name] for name in ("row", "col", "layer"))
    devices = mesh.devices.reshape(rows // CORES, CORES, cols, layers)
    cores = Mesh(devices, ("y", "core", "col", "layer"))
    row = ("y", "core")
    return jax.shard_map(
        functools.partial(on_device, dict(cores.shape)),
        mesh=cores,
        in_specs=(
            P("layer", row, "col"),
            P("layer", row, "col"),
            P("layer", row, "col"),
            P("layer", row, "col"),
            P(row),
            P("layer", None),
            P("col"),
        ),
        out_specs=P((*row, "layer"), "col"),
        check_vma=False,
    )
```

```python
import functools

import jax
import jax.numpy as jnp
from jax import lax
from jax.experimental import pallas as pl
from jax.experimental.pallas import tpu as pltpu
from jax.sharding import Mesh, PartitionSpec as P

BS = 256
CORES = 2
ROWS = 1024
HBM = pl.BlockSpec(memory_space=pl.ANY)
VMEM = pl.BlockSpec(memory_space=pltpu.VMEM)
PARAMS = pltpu.CompilerParams(vmem_limit_bytes=40 * 1024 * 1024)
SWAP = [(0, 1), (1, 0)]


def below(axis, size):
    return lax.broadcasted_iota(jnp.int32, (BS, BS), axis) < size


def masked(block, rows, columns):
    kept = jnp.where(below(0, rows) & below(1, columns), block.astype(jnp.float32), 0.0)
    return kept.astype(jnp.bfloat16)


def mask_kernel(*refs):
    count = 7
    a_out, b_out = refs[count : count + 2]
    slots, sems = refs[count + 2 : -1], refs[-1]
    copies = [pltpu.make_async_copy(refs[i], slots[i], sems.at[i]) for i in range(count)]
    for copy in copies:
        copy.start()
    for copy in copies:
        copy.wait()
    mask_a, mask_b, rows, inner, cols, a, b = slots
    columns = inner[0, lax.axis_index("col")]
    for i in range(ROWS // BS):
        place = slice(i * BS, (i + 1) * BS)
        a_out[place, :] = masked(a[0, place, :], rows[i] * mask_a[i], columns)
    first = (lax.axis_index("y") * CORES + lax.axis_index("core")) * mask_b.shape[1]
    for k in range(mask_b.shape[1]):
        for n in range(mask_b.shape[2]):
            place = (slice(k * BS, (k + 1) * BS), slice(n * BS, (n + 1) * BS))
            size = inner[0, first + k] * mask_b[0, k, n]
            b_out[place] = masked(b[(0,) + place], size, cols[n])


def product_kernel(steps, blocks, added, *refs):
    b_refs, refs = refs[:5], refs[5:]
    a_refs, refs = refs[: len(steps)], refs[len(steps) :]
    adds, (out_ref, a_all, b_all, extra, sems) = refs[:added], refs[added:]
    z, y, core = lax.axis_index("col"), lax.axis_index("y"), lax.axis_index("core")
    way = 2 * core - 1
    first, count = steps[0], len(steps)

    chips, mine, theirs = 4, core, 1 - core
    parts = (
        (0, 0, y, mine), (0, 1, y, theirs),
        (1, 0, y + way, mine), (1, 1, y + way, theirs),
        (2, 0, y - way, theirs), (2, 1, y - way, mine),
        (3, 0, y + 2, mine), (4, 0, y + 2, theirs),
    )
    for i, at, chip, owner in parts:
        for half in range(2):
            k = (lax.rem(chip + chips, chips) * CORES + owner) * 2 + half
            step = lax.rem(way * (k - z) + blocks, blocks)

            @pl.when((step >= first) & (step < first + count))
            def _(ref=b_refs[i], start=(at * 2 + half) * BS, step=step):
                pltpu.make_async_copy(
                    ref.at[pl.ds(start, BS)], b_all.at[step - first], sems.at[0]
                ).start()

    for i, ref in enumerate(a_refs):
        pltpu.make_async_copy(ref, a_all.at[:, pl.ds(i * BS, BS)], sems.at[1]).start()
    for i, ref in enumerate(adds):
        pltpu.make_async_copy(ref, extra.at[i], sems.at[2 + i]).start()
    pltpu.make_async_copy(b_all, b_all, sems.at[0]).wait()
    pltpu.make_async_copy(a_all, a_all, sems.at[1]).wait()
    for i, ref in enumerate(adds):
        pltpu.make_async_copy(ref, extra.at[i], sems.at[2 + i]).wait()

    b = b_all[...].reshape(count * BS, b_all.shape[2])
    for tile in range(ROWS // BS):
        rows = pl.ds(tile * BS, BS)
        total = jnp.dot(a_all[rows, :], b, preferred_element_type=jnp.float32)
        for i in range(added):
            total = total + extra[i, rows, :]
        out_ref[rows, :] = total


def layers_kernel(in_hbm, out_ref, parts, sem):
    copy = pltpu.make_async_copy(in_hbm, parts, sem)
    copy.start()
    copy.wait()
    out_ref[...] = (parts[0] + parts[1]) + (parts[2] + parts[3])


def after(value, earlier):
    return lax.optimization_barrier((value, earlier))[0]


def on_device(sizes, a_panel, b_panel, mask_a, mask_b, row_sizes, inner_sizes, col_sizes):
    cols, chips = sizes["col"], sizes["y"]
    width = b_panel.shape[2]
    ring = [
        (c * cols + i, c * cols + (i + (1, -1)[c]) % cols) for c in range(CORES) for i in range(cols)
    ]
    args = (mask_a.reshape(-1), mask_b, row_sizes, inner_sizes, col_sizes, a_panel, b_panel)
    own, b_eff = pl.pallas_call(
        mask_kernel,
        out_shape=tuple(
            jax.ShapeDtypeStruct(p.shape[1:], jnp.bfloat16) for p in (a_panel, b_panel)
        ),
        in_specs=[pl.BlockSpec(memory_space=pltpu.HBM)] * len(args),
        out_specs=(VMEM, VMEM),
        scratch_shapes=[pltpu.SMEM(x.shape, x.dtype) for x in args[:5]]
        + [pltpu.VMEM(x.shape, x.dtype) for x in args[5:]]
        + [pltpu.SemaphoreType.DMA((len(args),))],
        compiler_params=pltpu.CompilerParams(vmem_limit_bytes=60 * 1024 * 1024),
    )(*args)

    last = cols // 2
    held = [[own], [lax.ppermute(own, "core", SWAP)]]

    def product(steps, arrays, adds=()):
        n = len(steps)
        return pl.pallas_call(
            functools.partial(product_kernel, steps, cols, len(adds)),
            out_shape=jax.ShapeDtypeStruct((ROWS, width), jnp.float32),
            in_specs=[HBM] * (5 + len(arrays) + len(adds)),
            out_specs=VMEM,
            scratch_shapes=[
                pltpu.VMEM((ROWS, n * BS), jnp.bfloat16),
                pltpu.VMEM((n, BS, width), jnp.bfloat16),
                pltpu.VMEM((max(1, len(adds)), ROWS, width), jnp.float32),
                pltpu.SemaphoreType.DMA((2 + max(1, len(adds)),)),
            ],
            compiler_params=PARAMS,
            cost_estimate=pl.CostEstimate(
                flops=2 * ROWS * n * BS * width, bytes_accessed=2 * 2**20, transcendentals=0
            ),
        )(*b_all, *arrays, *adds)

    near_by = [
        (i * CORES + c, (i + (1, -1)[c]) % chips * CORES + c) for i in range(chips) for c in range(CORES)
    ]
    far_away = [(i, (i + 2) % chips) for i in range(chips)]
    b_all = [None] * 5
    b_other = others = None
    for step in range(1, last + 1):
        for j in range(2):
            if (step, j) == (last, 1):
                continue
            sent = held[j][-1]
            if step == last:
                shards = held[1][1 : last - 1]
                shards[-1] = after(shards[-1], sent)
                others = product(range(1, last - 1), shards)
                sent = after(sent, others)
            with jax.named_scope(f"stream_{j}_step_{step}"):
                held[j].append(lax.ppermute(sent, ("core", "col"), ring))
            if (step, j) == (1, 1):
                b_other = lax.ppermute(after(b_eff, own), "core", SWAP)
            if (step, j) == (2, 1):
                b_all[0] = jnp.concatenate([b_eff, after(b_other, sent)])
                b_all[1] = lax.ppermute(b_all[0], ("y", "core"), near_by)
            if (step, j) == (3, 1):
                b_all[3] = lax.ppermute(after(b_eff, sent), "y", far_away)
            if (step, j) == (5, 1):
                b_all[2] = lax.ppermute(after(b_all[1], sent), "core", SWAP)
            if (step, j) == (6, 1):
                b_all[4] = lax.ppermute(after(b_all[3], sent), "core", SWAP)

    others = product((last - 1,), held[1][last - 1 :], (others,))
    others = lax.ppermute(others, "core", SWAP)
    mine = product(range(last - 1), held[0][: last - 1])
    mine = product((last - 1,), held[0][last - 1 : last], (mine,))
    parts = product((last,), held[0][last:], (mine, others))
    parts = parts.reshape(-1, BS, width)
    parts = lax.all_to_all(parts, "layer", 0, 0)
    return pl.pallas_call(
        layers_kernel,
        out_shape=jax.ShapeDtypeStruct((BS, width), jnp.float32),
        in_specs=[HBM],
        out_specs=VMEM,
        scratch_shapes=[pltpu.VMEM(parts.shape, jnp.float32), pltpu.SemaphoreType.DMA],
        compiler_params=PARAMS,
    )(parts)


def solution(mesh):
    rows, cols, layers = (mesh.shape[name] for name in ("row", "col", "layer"))
    devices = mesh.devices.reshape(rows // CORES, CORES, cols, layers)
    cores = Mesh(devices, ("y", "core", "col", "layer"))
    row = ("y", "core")
    return jax.shard_map(
        functools.partial(on_device, dict(cores.shape)),
        mesh=cores,
        in_specs=(
            P("layer", row, "col"),
            P("layer", row, "col"),
            P("layer", row, "col"),
            P("layer", row, "col"),
            P(row),
            P("layer", None),
            P("col"),
        ),
        out_specs=P((*row, "layer"), "col"),
        check_vma=False,
    )
```

```python
import functools

import jax
import jax.numpy as jnp
from jax import lax
from jax.experimental import pallas as pl
from jax.experimental.pallas import tpu as pltpu
from jax.sharding import Mesh, PartitionSpec as P

BS = 256
CORES = 2
ROWS = 1024
HBM = pl.BlockSpec(memory_space=pl.ANY)
VMEM = pl.BlockSpec(memory_space=pltpu.VMEM)
PARAMS = pltpu.CompilerParams(vmem_limit_bytes=40 * 1024 * 1024)
SWAP = [(0, 1), (1, 0)]
STEP, CODES, CODE_ROWS = 12, 10, 16


def below(axis, size):
    return lax.broadcasted_iota(jnp.int32, (BS, BS), axis) < size


def masked(block, rows, columns):
    kept = jnp.where(below(0, rows) & below(1, columns), block.astype(jnp.float32), 0.0)
    return kept.astype(jnp.bfloat16)


def mask_kernel(*refs):
    count = 7
    a_out, b_out = refs[count : count + 2]
    slots, sems = refs[count + 2 : -1], refs[-1]
    copies = [pltpu.make_async_copy(refs[i], slots[i], sems.at[i]) for i in range(count)]
    for copy in copies:
        copy.start()
    for copy in copies:
        copy.wait()
    mask_a, mask_b, rows, inner, cols, a, b = slots
    columns = inner[0, lax.axis_index("col")]
    for i in range(ROWS // BS):
        place = slice(i * BS, (i + 1) * BS)
        a_out[place, :] = masked(a[0, place, :], rows[i] * mask_a[i], columns)
    first = (lax.axis_index("y") * CORES + lax.axis_index("core")) * mask_b.shape[1]
    for k in range(mask_b.shape[1]):
        for n in range(mask_b.shape[2]):
            place = (slice(k * BS, (k + 1) * BS), slice(n * BS, (n + 1) * BS))
            size = inner[0, first + k] * mask_b[0, k, n]
            b_out[place] = masked(b[(0,) + place], size, cols[n])


def product_kernel(steps, blocks, added, *refs):
    b_refs, refs = refs[:5], refs[5:]
    a_refs, refs = refs[: len(steps)], refs[len(steps) :]
    adds, (out_ref, a_all, b_all, extra, sems) = refs[:added], refs[added:]
    z, y, core = lax.axis_index("col"), lax.axis_index("y"), lax.axis_index("core")
    way = 2 * core - 1
    first, count = steps[0], len(steps)

    chips, mine, theirs = 4, core, 1 - core
    parts = (
        (0, 0, y, mine), (0, 1, y, theirs),
        (1, 0, y + way, mine), (1, 1, y + way, theirs),
        (2, 0, y - way, theirs), (2, 1, y - way, mine),
        (3, 0, y + 2, mine), (4, 0, y + 2, theirs),
    )
    for i, at, chip, owner in parts:
        for half in range(2):
            k = (lax.rem(chip + chips, chips) * CORES + owner) * 2 + half
            step = lax.rem(way * (k - z) + blocks, blocks)

            @pl.when((step >= first) & (step < first + count))
            def _(ref=b_refs[i], start=(at * 2 + half) * BS, step=step):
                pltpu.make_async_copy(
                    ref.at[pl.ds(start, BS)], b_all.at[step - first], sems.at[0]
                ).start()

    for i, ref in enumerate(a_refs):
        pltpu.make_async_copy(ref, a_all.at[:, pl.ds(i * BS, BS)], sems.at[1]).start()
    for i, ref in enumerate(adds):
        pltpu.make_async_copy(ref, extra.at[i], sems.at[2 + i]).start()
    pltpu.make_async_copy(b_all, b_all, sems.at[0]).wait()
    pltpu.make_async_copy(a_all, a_all, sems.at[1]).wait()
    for i, ref in enumerate(adds):
        pltpu.make_async_copy(ref, extra.at[i], sems.at[2 + i]).wait()

    b = b_all[...].reshape(count * BS, b_all.shape[2])
    for tile in range(ROWS // BS):
        rows = pl.ds(tile * BS, BS)
        total = jnp.dot(a_all[rows, :], b, preferred_element_type=jnp.float32)
        for i in range(added):
            total = total + extra[i, rows, :]
        if len(out_ref.shape) == 2:
            out_ref[rows, :] = total
        else:
            encode(total, out_ref.at[tile])


def encode(total, out_ref):
    top = jnp.max(jnp.abs(total), keepdims=True)
    scale, code = jnp.ones_like(top), jnp.zeros_like(top)
    for c in range(1, CODES + 1):
        small = top < 2.0 ** (14 - STEP * c)
        scale = jnp.where(small, 2.0 ** (STEP * c), scale)
        code = jnp.where(small, float(c), code)
    out_ref[:BS, :] = total * scale
    out_ref[BS:, :] = jnp.broadcast_to(code, (CODE_ROWS, total.shape[1]))


def decoded(parts):
    code = parts[:, BS:, :1].astype(jnp.float32).max(axis=1, keepdims=True)
    scale = jnp.ones_like(code)
    for c in range(1, CODES + 1):
        scale = jnp.where(code > c - 0.5, 2.0 ** (-STEP * c), scale)
    return parts[:, :BS].astype(jnp.float32) * scale


def after(value, earlier):
    return lax.optimization_barrier((value, earlier))[0]


def on_device(sizes, a_panel, b_panel, mask_a, mask_b, row_sizes, inner_sizes, col_sizes):
    cols, chips = sizes["col"], sizes["y"]
    width = b_panel.shape[2]
    ring = [
        (c * cols + i, c * cols + (i + (1, -1)[c]) % cols) for c in range(CORES) for i in range(cols)
    ]
    args = (mask_a.reshape(-1), mask_b, row_sizes, inner_sizes, col_sizes, a_panel, b_panel)
    own, b_eff = pl.pallas_call(
        mask_kernel,
        out_shape=tuple(
            jax.ShapeDtypeStruct(p.shape[1:], jnp.bfloat16) for p in (a_panel, b_panel)
        ),
        in_specs=[pl.BlockSpec(memory_space=pltpu.HBM)] * len(args),
        out_specs=(VMEM, VMEM),
        scratch_shapes=[pltpu.SMEM(x.shape, x.dtype) for x in args[:5]]
        + [pltpu.VMEM(x.shape, x.dtype) for x in args[5:]]
        + [pltpu.SemaphoreType.DMA((len(args),))],
        compiler_params=pltpu.CompilerParams(vmem_limit_bytes=60 * 1024 * 1024),
    )(*args)

    last = cols // 2
    held = [[own], [lax.ppermute(own, "core", SWAP)]]

    def product(steps, arrays, adds=(), coded=False):
        n = len(steps)
        return pl.pallas_call(
            functools.partial(product_kernel, steps, cols, len(adds)),
            out_shape=jax.ShapeDtypeStruct((ROWS // BS, BS + CODE_ROWS, width), jnp.float32)
            if coded
            else jax.ShapeDtypeStruct((ROWS, width), jnp.float32),
            in_specs=[HBM] * (5 + len(arrays) + len(adds)),
            out_specs=VMEM,
            scratch_shapes=[
                pltpu.VMEM((ROWS, n * BS), jnp.bfloat16),
                pltpu.VMEM((n, BS, width), jnp.bfloat16),
                pltpu.VMEM((max(1, len(adds)), ROWS, width), jnp.float32),
                pltpu.SemaphoreType.DMA((2 + max(1, len(adds)),)),
            ],
            compiler_params=PARAMS,
            cost_estimate=pl.CostEstimate(
                flops=2 * ROWS * n * BS * width, bytes_accessed=2 * 2**20, transcendentals=0
            ),
        )(*b_all, *arrays, *adds)

    near_by = [
        (i * CORES + c, (i + (1, -1)[c]) % chips * CORES + c) for i in range(chips) for c in range(CORES)
    ]
    far_away = [(i, (i + 2) % chips) for i in range(chips)]
    b_all = [None] * 5
    b_other = None
    turned = []
    for step in range(1, last + 1):
        for j in range(2):
            if (step, j) == (last, 1):
                continue
            sent = held[j][-1]
            if j == 1 and step > 4:
                sent = after(sent, turned[step - 5])
            with jax.named_scope(f"stream_{j}_step_{step}"):
                held[j].append(lax.ppermute(sent, ("core", "col"), ring))
            if j == 1 and step > 1:
                turned.append(lax.ppermute(held[1][step - 1], "core", SWAP))
            if (step, j) == (1, 1):
                b_other = lax.ppermute(after(b_eff, sent), "core", SWAP)
            if (step, j) == (2, 1):
                b_all[0] = jnp.concatenate([b_eff, after(b_other, sent)])
                b_all[1] = lax.ppermute(b_all[0], ("y", "core"), near_by)
            if (step, j) == (3, 1):
                b_all[3] = lax.ppermute(after(b_eff, sent), "y", far_away)
            if (step, j) == (5, 1):
                b_all[2] = lax.ppermute(after(b_all[1], sent), "core", SWAP)
            if (step, j) == (6, 0):
                b_all[4] = lax.ppermute(after(b_all[3], sent), "core", SWAP)
    turned.append(lax.ppermute(held[1][last - 1], "core", SWAP))

    shards = held[0] + turned[::-1]
    near = product(range(last - 1), shards[: last - 1])
    across = product(range(last + 2, cols), shards[last + 2 :])
    steps = range(last - 1, last + 2)
    parts = product(steps, [shards[s] for s in steps], (near, across), True)
    parts = parts.astype(jnp.float16)
    return decoded(lax.all_to_all(parts, "layer", 0, 0)).sum(axis=0)


def solution(mesh):
    rows, cols, layers = (mesh.shape[name] for name in ("row", "col", "layer"))
    devices = mesh.devices.reshape(rows // CORES, CORES, cols, layers)
    cores = Mesh(devices, ("y", "core", "col", "layer"))
    row = ("y", "core")
    return jax.shard_map(
        functools.partial(on_device, dict(cores.shape)),
        mesh=cores,
        in_specs=(
            P("layer", row, "col"),
            P("layer", row, "col"),
            P("layer", row, "col"),
            P("layer", row, "col"),
            P(row),
            P("layer", None),
            P("col"),
        ),
        out_specs=P((*row, "layer"), "col"),
        check_vma=False,
    )
```

```python
import functools

import jax
import jax.numpy as jnp
from jax import lax
from jax.experimental import pallas as pl
from jax.experimental.pallas import tpu as pltpu
from jax.sharding import Mesh, PartitionSpec as P

BS = 256
CORES = 2
ROWS = 1024
HBM = pl.BlockSpec(memory_space=pl.ANY)
VMEM = pl.BlockSpec(memory_space=pltpu.VMEM)
PARAMS = pltpu.CompilerParams(vmem_limit_bytes=40 * 1024 * 1024)
SWAP = [(0, 1), (1, 0)]
STEP, CODES, CODE_ROWS = 12, 10, 16


def below(axis, size):
    return lax.broadcasted_iota(jnp.int32, (BS, BS), axis) < size


def masked(block, rows, columns):
    kept = jnp.where(below(0, rows) & below(1, columns), block.astype(jnp.float32), 0.0)
    return kept.astype(jnp.bfloat16)


def fetched(refs):
    sems, refs = refs[-1], refs[:-1]
    count = len(refs) // 2
    copies = [pltpu.make_async_copy(refs[i], refs[count + 1 + i], sems.at[i]) for i in range(count)]
    for copy in copies:
        copy.start()
    for copy in copies:
        copy.wait()
    return refs[count], refs[count + 1 :]


def mask_a_kernel(*refs):
    out_ref, (mask, rows, inner, a) = fetched(refs)
    columns = inner[0, lax.axis_index("col")]
    for i in range(ROWS // BS):
        place = slice(i * BS, (i + 1) * BS)
        out_ref[place, :] = masked(a[0, place, :], rows[i] * mask[i], columns)


def mask_b_kernel(*refs):
    out_ref, (mask, inner, cols, b) = fetched(refs)
    first = (lax.axis_index("y") * CORES + lax.axis_index("core")) * mask.shape[1]
    for k in range(mask.shape[1]):
        for n in range(mask.shape[2]):
            place = (slice(k * BS, (k + 1) * BS), slice(n * BS, (n + 1) * BS))
            size = inner[0, first + k] * mask[0, k, n]
            out_ref[place] = masked(b[(0,) + place], size, cols[n])


def mask_call(kernel, shape, *args):
    spaces = [pltpu.SMEM] * (len(args) - 1) + [pltpu.VMEM]
    return pl.pallas_call(
        kernel,
        out_shape=jax.ShapeDtypeStruct(shape, jnp.bfloat16),
        in_specs=[pl.BlockSpec(memory_space=pltpu.HBM)] * len(args),
        out_specs=VMEM,
        scratch_shapes=[s(x.shape, x.dtype) for s, x in zip(spaces, args)]
        + [pltpu.SemaphoreType.DMA((len(args),))],
        compiler_params=pltpu.CompilerParams(vmem_limit_bytes=60 * 1024 * 1024),
    )(*args)


def product_kernel(steps, blocks, added, *refs):
    b_refs, refs = refs[:4], refs[4:]
    a_refs, refs = refs[: len(steps)], refs[len(steps) :]
    adds, refs = refs[:added], refs[added:]
    outs, (a_all, b_all, extra, sems) = refs[:-4], refs[-4:]
    out_ref, own_ref = outs[0], outs[-1]
    z, y, core = lax.axis_index("col"), lax.axis_index("y"), lax.axis_index("core")
    way = 2 * core - 1
    first, count = steps[0], len(steps)

    chips, mine, theirs = 4, core, 1 - core
    parts = (
        (0, 0, y, mine), (0, 1, y, theirs),
        (1, 0, y + way, mine), (1, 1, y + way, theirs),
        (2, 0, y - way, theirs), (2, 1, y - way, mine),
        (3, 0, y + 2, mine), (3, 1, y + 2, theirs),
    )
    for i, at, chip, owner in parts:
        for half in range(2):
            k = (lax.rem(chip + chips, chips) * CORES + owner) * 2 + half
            step = lax.rem(way * (k - z) + blocks, blocks)

            @pl.when((step >= first) & (step < first + count))
            def _(ref=b_refs[i], start=(at * 2 + half) * BS, step=step):
                pltpu.make_async_copy(
                    ref.at[pl.ds(start, BS)], b_all.at[step - first], sems.at[0]
                ).start()

    for i, ref in enumerate(a_refs):
        pltpu.make_async_copy(ref, a_all.at[:, pl.ds(i * BS, BS)], sems.at[1]).start()
    for i, ref in enumerate(adds):
        pltpu.make_async_copy(ref, extra.at[i], sems.at[2 + i]).start()
    pltpu.make_async_copy(b_all, b_all, sems.at[0]).wait()
    pltpu.make_async_copy(a_all, a_all, sems.at[1]).wait()
    for i, ref in enumerate(adds):
        pltpu.make_async_copy(ref, extra.at[i], sems.at[2 + i]).wait()

    b = b_all[...].reshape(count * BS, b_all.shape[2])
    for tile in range(ROWS // BS):
        rows = pl.ds(tile * BS, BS)
        total = jnp.dot(a_all[rows, :], b, preferred_element_type=jnp.float32)
        for i in range(added):
            total = total + extra[i, rows, :]
        if len(outs) == 1:
            out_ref[rows, :] = total
        else:
            encode(total, out_ref.at[tile])

            @pl.when(lax.axis_index("layer") == tile)
            def _(total=total):
                own_ref[...] = total


def encode(total, out_ref):
    top = jnp.max(jnp.abs(total), keepdims=True)
    scale, code = jnp.ones_like(top), jnp.zeros_like(top)
    for c in range(1, CODES + 1):
        small = top < 2.0 ** (14 - STEP * c)
        scale = jnp.where(small, 2.0 ** (STEP * c), scale)
        code = jnp.where(small, float(c), code)
    out_ref[:BS, :] = total * scale
    out_ref[BS:, :] = jnp.broadcast_to(code, (CODE_ROWS, total.shape[1]))


def decoded(parts, own):
    code = parts[:, BS:, :1].astype(jnp.float32).max(axis=1, keepdims=True)
    scale = jnp.ones_like(code)
    for c in range(1, CODES + 1):
        scale = jnp.where(code > c - 0.5, 2.0 ** (-STEP * c), scale)
    scale = jnp.where(jnp.arange(parts.shape[0])[:, None, None] == own, 0.0, scale)
    return parts[:, :BS].astype(jnp.float32) * scale


def after(value, earlier):
    return lax.optimization_barrier((value, earlier))[0]


def on_device(sizes, a_panel, b_panel, mask_a, mask_b, row_sizes, inner_sizes, col_sizes):
    cols, chips = sizes["col"], sizes["y"]
    width = b_panel.shape[2]
    ring = [
        (c * cols + i, c * cols + (i + (1, -1)[c]) % cols) for c in range(CORES) for i in range(cols)
    ]
    own = mask_call(
        mask_a_kernel, a_panel.shape[1:], mask_a.reshape(-1), row_sizes, inner_sizes, a_panel
    )
    last = cols // 2
    held = [[own], [lax.ppermute(own, "core", SWAP)]]

    def product(steps, arrays, adds=(), coded=False):
        n = len(steps)
        return pl.pallas_call(
            functools.partial(product_kernel, steps, cols, len(adds)),
            out_shape=(
                jax.ShapeDtypeStruct((ROWS // BS, BS + CODE_ROWS, width), jnp.float32),
                jax.ShapeDtypeStruct((BS, width), jnp.float32),
            )
            if coded
            else jax.ShapeDtypeStruct((ROWS, width), jnp.float32),
            in_specs=[HBM] * (4 + len(arrays) + len(adds)),
            out_specs=(VMEM, VMEM) if coded else VMEM,
            scratch_shapes=[
                pltpu.VMEM((ROWS, n * BS), jnp.bfloat16),
                pltpu.VMEM((n, BS, width), jnp.bfloat16),
                pltpu.VMEM((max(1, len(adds)), ROWS, width), jnp.float32),
                pltpu.SemaphoreType.DMA((2 + max(1, len(adds)),)),
            ],
            compiler_params=PARAMS,
            cost_estimate=pl.CostEstimate(
                flops=2 * ROWS * n * BS * width, bytes_accessed=2 * 2**20, transcendentals=0
            ),
        )(*b_all, *arrays, *adds)

    near_by = [
        (i * CORES + c, (i + (1, -1)[c]) % chips * CORES + c) for i in range(chips) for c in range(CORES)
    ]
    b_eff = b_other = None
    b_all = [None] * 4
    turned = []
    for step in range(1, last + 1):
        for j in range(2):
            if (step, j) == (last, 1):
                continue
            sent = held[j][-1]
            with jax.named_scope(f"stream_{j}_step_{step}"):
                held[j].append(lax.ppermute(sent, ("core", "col"), ring))
            if (step, j) == (1, 0):
                sizes_k = after(inner_sizes, held[0][1])
                b_eff = mask_call(
                    mask_b_kernel, b_panel.shape[1:], mask_b, sizes_k, col_sizes, b_panel
                )
            if (step, j) == (1, 1):
                with jax.named_scope("b_swap"):
                    b_other = lax.ppermute(b_eff, "core", SWAP)
            if (step, j) == (2, 1):
                b_all[0] = jnp.concatenate([b_eff, after(b_other, sent)])
                with jax.named_scope("b_near"):
                    b_all[1] = lax.ppermute(b_all[0], ("y", "core"), near_by)
            if (step, j) == (3, 1):
                with jax.named_scope("b_far"):
                    b_all[3] = lax.ppermute(after(b_all[1], sent), ("y", "core"), near_by)
            if (step, j) == (5, 1):
                with jax.named_scope("b_turn"):
                    b_all[2] = lax.ppermute(after(b_all[1], sent), "core", SWAP)
            if j == 1 and step > 1:
                turned.append(lax.ppermute(held[1][step - 1], "core", SWAP))
    turned.append(lax.ppermute(held[1][last - 1], "core", SWAP))

    shards = held[0] + turned[::-1]
    near = product(range(last - 1), shards[: last - 1])
    across = product(range(last + 3, cols), shards[last + 3 :])
    steps = range(last - 1, last + 3)
    parts, mine = product(steps, [shards[s] for s in steps], (near, across), True)
    parts = parts.astype(jnp.float16)
    parts = decoded(lax.all_to_all(parts, "layer", 0, 0), lax.axis_index("layer"))
    return mine + parts.sum(axis=0)


def solution(mesh):
    rows, cols, layers = (mesh.shape[name] for name in ("row", "col", "layer"))
    devices = mesh.devices.reshape(rows // CORES, CORES, cols, layers)
    cores = Mesh(devices, ("y", "core", "col", "layer"))
    row = ("y", "core")
    return jax.shard_map(
        functools.partial(on_device, dict(cores.shape)),
        mesh=cores,
        in_specs=(
            P("layer", row, "col"),
            P("layer", row, "col"),
            P("layer", row, "col"),
            P("layer", row, "col"),
            P(row),
            P("layer", None),
            P("col"),
        ),
        out_specs=P((*row, "layer"), "col"),
        check_vma=False,
    )
```

```python
import functools

import jax
import jax.numpy as jnp
from jax import lax
from jax.experimental import pallas as pl
from jax.experimental.pallas import tpu as pltpu
from jax.sharding import Mesh, PartitionSpec as P

BS = 256
CORES = 2
ROWS = 1024
HBM = pl.BlockSpec(memory_space=pl.ANY)
VMEM = pl.BlockSpec(memory_space=pltpu.VMEM)
PARAMS = pltpu.CompilerParams(vmem_limit_bytes=40 * 1024 * 1024)
SWAP = [(0, 1), (1, 0)]
STEP, CODES, CODE_ROWS = 12, 10, 16


def below(axis, size):
    return lax.broadcasted_iota(jnp.int32, (BS, BS), axis) < size


def masked(block, rows, columns):
    kept = jnp.where(below(0, rows) & below(1, columns), block.astype(jnp.float32), 0.0)
    return kept.astype(jnp.bfloat16)


def fetched(refs):
    sems, refs = refs[-1], refs[:-1]
    count = len(refs) // 2
    copies = [pltpu.make_async_copy(refs[i], refs[count + 1 + i], sems.at[i]) for i in range(count)]
    for copy in copies:
        copy.start()
    for copy in copies:
        copy.wait()
    return refs[count], refs[count + 1 :]


def mask_a_kernel(*refs):
    out_ref, (mask, rows, inner, a) = fetched(refs)
    columns = inner[0, lax.axis_index("col")]
    for i in range(ROWS // BS):
        place = slice(i * BS, (i + 1) * BS)
        out_ref[place, :] = masked(a[0, place, :], rows[i] * mask[i], columns)


def mask_b_kernel(*refs):
    out_ref, (mask, inner, cols, b) = fetched(refs)
    first = (lax.axis_index("y") * CORES + lax.axis_index("core")) * mask.shape[1]
    for k in range(mask.shape[1]):
        for n in range(mask.shape[2]):
            place = (slice(k * BS, (k + 1) * BS), slice(n * BS, (n + 1) * BS))
            size = inner[0, first + k] * mask[0, k, n]
            out_ref[place] = masked(b[(0,) + place], size, cols[n])


def mask_call(kernel, shape, *args):
    spaces = [pltpu.SMEM] * (len(args) - 1) + [pltpu.VMEM]
    return pl.pallas_call(
        kernel,
        out_shape=jax.ShapeDtypeStruct(shape, jnp.bfloat16),
        in_specs=[pl.BlockSpec(memory_space=pltpu.HBM)] * len(args),
        out_specs=VMEM,
        scratch_shapes=[s(x.shape, x.dtype) for s, x in zip(spaces, args)]
        + [pltpu.SemaphoreType.DMA((len(args),))],
        compiler_params=pltpu.CompilerParams(vmem_limit_bytes=60 * 1024 * 1024),
    )(*args)


def product_kernel(steps, blocks, added, *refs):
    b_refs, refs = refs[:4], refs[4:]
    a_refs, refs = refs[: len(steps)], refs[len(steps) :]
    adds, (out_ref, a_all, b_all, extra, sems) = refs[:added], refs[added:]
    z, y, core = lax.axis_index("col"), lax.axis_index("y"), lax.axis_index("core")
    way = 2 * core - 1
    first, count = steps[0], len(steps)

    chips, mine, theirs = 4, core, 1 - core
    parts = (
        (0, 0, y, mine), (0, 1, y, theirs),
        (1, 0, y + way, mine), (1, 1, y + way, theirs),
        (2, 0, y - way, theirs), (2, 1, y - way, mine),
        (3, 0, y + 2, mine), (3, 1, y + 2, theirs),
    )
    for i, at, chip, owner in parts:
        for half in range(2):
            k = (lax.rem(chip + chips, chips) * CORES + owner) * 2 + half
            step = lax.rem(way * (k - z) + blocks, blocks)

            @pl.when((step >= first) & (step < first + count))
            def _(ref=b_refs[i], start=(at * 2 + half) * BS, step=step):
                pltpu.make_async_copy(
                    ref.at[pl.ds(start, BS)], b_all.at[step - first], sems.at[0]
                ).start()

    for i, ref in enumerate(a_refs):
        pltpu.make_async_copy(ref, a_all.at[:, pl.ds(i * BS, BS)], sems.at[1]).start()
    for i, ref in enumerate(adds):
        pltpu.make_async_copy(ref, extra.at[i], sems.at[2 + i]).start()
    pltpu.make_async_copy(b_all, b_all, sems.at[0]).wait()
    pltpu.make_async_copy(a_all, a_all, sems.at[1]).wait()
    for i, ref in enumerate(adds):
        pltpu.make_async_copy(ref, extra.at[i], sems.at[2 + i]).wait()

    b = b_all[...].reshape(count * BS, b_all.shape[2])
    for tile in range(ROWS // BS):
        rows = pl.ds(tile * BS, BS)
        total = jnp.dot(a_all[rows, :], b, preferred_element_type=jnp.float32)
        for i in range(added):
            total = total + extra[i, rows, :]
        if len(out_ref.shape) == 2:
            out_ref[rows, :] = total
        else:
            encode(total, out_ref.at[tile])


def encode(total, out_ref):
    top = jnp.max(jnp.abs(total), keepdims=True)
    scale, code = jnp.ones_like(top), jnp.zeros_like(top)
    for c in range(1, CODES + 1):
        small = top < 2.0 ** (14 - STEP * c)
        scale = jnp.where(small, 2.0 ** (STEP * c), scale)
        code = jnp.where(small, float(c), code)
    out_ref[:BS, :] = total * scale
    out_ref[BS:, :] = jnp.broadcast_to(code, (CODE_ROWS, total.shape[1]))


def decoded(parts):
    code = parts[:, BS:, :1].astype(jnp.float32).max(axis=1, keepdims=True)
    scale = jnp.ones_like(code)
    for c in range(1, CODES + 1):
        scale = jnp.where(code > c - 0.5, 2.0 ** (-STEP * c), scale)
    return parts[:, :BS].astype(jnp.float32) * scale


def after(value, earlier):
    return lax.optimization_barrier((value, earlier))[0]


def on_device(sizes, a_panel, b_panel, mask_a, mask_b, row_sizes, inner_sizes, col_sizes):
    cols, chips = sizes["col"], sizes["y"]
    width = b_panel.shape[2]
    ring = [
        (c * cols + i, c * cols + (i + (1, -1)[c]) % cols) for c in range(CORES) for i in range(cols)
    ]
    own = mask_call(
        mask_a_kernel, a_panel.shape[1:], mask_a.reshape(-1), row_sizes, inner_sizes, a_panel
    )

    last = cols // 2
    held = [[own], [lax.ppermute(own, "core", SWAP)]]

    def product(steps, arrays, adds=(), coded=False):
        n = len(steps)
        return pl.pallas_call(
            functools.partial(product_kernel, steps, cols, len(adds)),
            out_shape=jax.ShapeDtypeStruct((ROWS // BS, BS + CODE_ROWS, width), jnp.float32)
            if coded
            else jax.ShapeDtypeStruct((ROWS, width), jnp.float32),
            in_specs=[HBM] * (4 + len(arrays) + len(adds)),
            out_specs=VMEM,
            scratch_shapes=[
                pltpu.VMEM((ROWS, n * BS), jnp.bfloat16),
                pltpu.VMEM((n, BS, width), jnp.bfloat16),
                pltpu.VMEM((max(1, len(adds)), ROWS, width), jnp.float32),
                pltpu.SemaphoreType.DMA((2 + max(1, len(adds)),)),
            ],
            compiler_params=PARAMS,
            cost_estimate=pl.CostEstimate(
                flops=2 * ROWS * n * BS * width, bytes_accessed=2 * 2**20, transcendentals=0
            ),
        )(*b_all, *arrays, *adds)

    near_by = [
        (i * CORES + c, (i + (1, -1)[c]) % chips * CORES + c) for i in range(chips) for c in range(CORES)
    ]
    b_eff = b_turned = None
    b_all = [None] * 4
    turned = []
    for step in range(1, last + 1):
        for j in range(2):
            if (step, j) == (last, 1):
                continue
            sent = held[j][-1]
            if (step, j) == (6, 0):
                sent = after(sent, b_all[2])
            if j == 1 and step > 3:
                sent = after(sent, turned[step - 4])
            with jax.named_scope(f"stream_{j}_step_{step}"):
                held[j].append(lax.ppermute(sent, ("core", "col"), ring))
            if (step, j) == (1, 0):
                sizes_k = after(inner_sizes, held[1][0])
                b_eff = mask_call(
                    mask_b_kernel, b_panel.shape[1:], mask_b, sizes_k, col_sizes, b_panel
                )
            if (step, j) == (1, 1):
                with jax.named_scope("b_swap"):
                    b_turned = lax.ppermute(b_eff, "core", SWAP)
            if (step, j) == (2, 1):
                b_all[0] = jnp.concatenate([b_eff, b_turned])
                with jax.named_scope("b_near"):
                    b_all[1] = lax.ppermute(b_all[0], ("y", "core"), near_by)
            if (step, j) == (3, 1):
                with jax.named_scope("b_far"):
                    b_all[3] = lax.ppermute(b_all[1], ("y", "core"), near_by)
            if (step, j) == (4, 0):
                with jax.named_scope("b_turn"):
                    b_all[2] = lax.ppermute(after(b_all[1], sent), "core", SWAP)
            if j == 1 and step > 1:
                turned.append(lax.ppermute(after(held[1][step - 1], sent), "core", SWAP))
    turned.append(lax.ppermute(held[1][last - 1], "core", SWAP))

    shards = held[0] + turned[::-1]
    near = product(range(last - 1), shards[: last - 1])
    across = product(range(last + 2, cols), shards[last + 2 :])
    steps = range(last - 1, last + 2)
    parts = product(steps, [shards[s] for s in steps], (near, across), True)
    parts = parts.astype(jnp.float16)
    return decoded(lax.all_to_all(parts, "layer", 0, 0)).sum(axis=0)


def solution(mesh):
    rows, cols, layers = (mesh.shape[name] for name in ("row", "col", "layer"))
    devices = mesh.devices.reshape(rows // CORES, CORES, cols, layers)
    cores = Mesh(devices, ("y", "core", "col", "layer"))
    row = ("y", "core")
    return jax.shard_map(
        functools.partial(on_device, dict(cores.shape)),
        mesh=cores,
        in_specs=(
            P("layer", row, "col"),
            P("layer", row, "col"),
            P("layer", row, "col"),
            P("layer", row, "col"),
            P(row),
            P("layer", None),
            P("col"),
        ),
        out_specs=P((*row, "layer"), "col"),
        check_vma=False,
    )
```

```python
import functools

import jax
import jax.numpy as jnp
from jax import lax
from jax.experimental import pallas as pl
from jax.experimental.pallas import tpu as pltpu
from jax.sharding import Mesh, PartitionSpec as P

BS = 256
CORES = 2
ROWS = 1024
HBM = pl.BlockSpec(memory_space=pl.ANY)
VMEM = pl.BlockSpec(memory_space=pltpu.VMEM)
PARAMS = pltpu.CompilerParams(vmem_limit_bytes=40 * 1024 * 1024)
SWAP = [(0, 1), (1, 0)]
STEP, CODES, CODE_ROWS = 12, 10, 16


def below(axis, size):
    return lax.broadcasted_iota(jnp.int32, (BS, BS), axis) < size


def masked(block, rows, columns):
    kept = jnp.where(below(0, rows) & below(1, columns), block.astype(jnp.float32), 0.0)
    return kept.astype(jnp.bfloat16)


def fetched(refs):
    sems, refs = refs[-1], refs[:-1]
    count = len(refs) // 2
    copies = [pltpu.make_async_copy(refs[i], refs[count + 1 + i], sems.at[i]) for i in range(count)]
    for copy in copies:
        copy.start()
    for copy in copies:
        copy.wait()
    return refs[count], refs[count + 1 :]


def mask_a_kernel(*refs):
    out_ref, (mask, rows, inner, a) = fetched(refs)
    columns = inner[0, lax.axis_index("col")]
    for i in range(ROWS // BS):
        place = slice(i * BS, (i + 1) * BS)
        out_ref[place, :] = masked(a[0, place, :], rows[i] * mask[i], columns)


def mask_b_kernel(*refs):
    out_ref, (mask, inner, cols, b) = fetched(refs)
    first = (lax.axis_index("y") * CORES + lax.axis_index("core")) * mask.shape[1]
    for k in range(mask.shape[1]):
        for n in range(mask.shape[2]):
            place = (slice(k * BS, (k + 1) * BS), slice(n * BS, (n + 1) * BS))
            size = inner[0, first + k] * mask[0, k, n]
            out_ref[place] = masked(b[(0,) + place], size, cols[n])


def mask_call(kernel, shape, *args):
    spaces = [pltpu.SMEM] * (len(args) - 1) + [pltpu.VMEM]
    return pl.pallas_call(
        kernel,
        out_shape=jax.ShapeDtypeStruct(shape, jnp.bfloat16),
        in_specs=[pl.BlockSpec(memory_space=pltpu.HBM)] * len(args),
        out_specs=VMEM,
        scratch_shapes=[s(x.shape, x.dtype) for s, x in zip(spaces, args)]
        + [pltpu.SemaphoreType.DMA((len(args),))],
        compiler_params=pltpu.CompilerParams(vmem_limit_bytes=60 * 1024 * 1024),
    )(*args)


def product_kernel(steps, blocks, added, *refs):
    b_refs, refs = refs[:4], refs[4:]
    a_refs, refs = refs[: len(steps)], refs[len(steps) :]
    adds, (out_ref, a_all, b_all, extra, sems) = refs[:added], refs[added:]
    z, y, core = lax.axis_index("col"), lax.axis_index("y"), lax.axis_index("core")
    way = 2 * core - 1
    first, count = steps[0], len(steps)

    chips, mine, theirs = 4, core, 1 - core
    parts = (
        (0, 0, y, mine), (0, 1, y, theirs),
        (1, 0, y + way, mine), (1, 1, y + way, theirs),
        (2, 0, y - way, theirs), (2, 1, y - way, mine),
        (3, 0, y + 2, mine), (3, 1, y + 2, theirs),
    )
    for i, at, chip, owner in parts:
        for half in range(2):
            k = (lax.rem(chip + chips, chips) * CORES + owner) * 2 + half
            step = lax.rem(way * (k - z) + blocks, blocks)

            @pl.when((step >= first) & (step < first + count))
            def _(ref=b_refs[i], start=(at * 2 + half) * BS, step=step):
                pltpu.make_async_copy(
                    ref.at[pl.ds(start, BS)], b_all.at[step - first], sems.at[0]
                ).start()

    for i, ref in enumerate(a_refs):
        pltpu.make_async_copy(ref, a_all.at[:, pl.ds(i * BS, BS)], sems.at[1]).start()
    for i, ref in enumerate(adds):
        pltpu.make_async_copy(ref, extra.at[i], sems.at[2 + i]).start()
    pltpu.make_async_copy(b_all, b_all, sems.at[0]).wait()
    pltpu.make_async_copy(a_all, a_all, sems.at[1]).wait()
    for i, ref in enumerate(adds):
        pltpu.make_async_copy(ref, extra.at[i], sems.at[2 + i]).wait()

    b = b_all[...].reshape(count * BS, b_all.shape[2])
    for tile in range(ROWS // BS):
        rows = pl.ds(tile * BS, BS)
        total = jnp.dot(a_all[rows, :], b, preferred_element_type=jnp.float32)
        for i in range(added):
            total = total + extra[i, rows, :]
        if len(out_ref.shape) == 2:
            out_ref[rows, :] = total
        else:
            encode(total, out_ref.at[tile])


def encode(total, out_ref):
    top = jnp.max(jnp.abs(total), keepdims=True)
    scale, code = jnp.ones_like(top), jnp.zeros_like(top)
    for c in range(1, CODES + 1):
        small = top < 2.0 ** (14 - STEP * c)
        scale = jnp.where(small, 2.0 ** (STEP * c), scale)
        code = jnp.where(small, float(c), code)
    out_ref[:BS, :] = total * scale
    out_ref[BS:, :] = jnp.broadcast_to(code, (CODE_ROWS, total.shape[1]))


def decoded(parts):
    code = parts[:, BS:, :1].astype(jnp.float32).max(axis=1, keepdims=True)
    scale = jnp.ones_like(code)
    for c in range(1, CODES + 1):
        scale = jnp.where(code > c - 0.5, 2.0 ** (-STEP * c), scale)
    return parts[:, :BS].astype(jnp.float32) * scale


def after(value, earlier):
    return lax.optimization_barrier((value, earlier))[0]


def on_device(sizes, a_panel, b_panel, mask_a, mask_b, row_sizes, inner_sizes, col_sizes):
    cols, chips = sizes["col"], sizes["y"]
    width = b_panel.shape[2]
    ring = [
        (c * cols + i, c * cols + (i + (1, -1)[c]) % cols) for c in range(CORES) for i in range(cols)
    ]
    own = mask_call(
        mask_a_kernel, a_panel.shape[1:], mask_a.reshape(-1), row_sizes, inner_sizes, a_panel
    )

    last = cols // 2
    held = [[own], [lax.ppermute(own, "core", SWAP)]]

    def product(steps, arrays, adds=(), coded=False):
        n = len(steps)
        return pl.pallas_call(
            functools.partial(product_kernel, steps, cols, len(adds)),
            out_shape=jax.ShapeDtypeStruct((ROWS // BS, BS + CODE_ROWS, width), jnp.float32)
            if coded
            else jax.ShapeDtypeStruct((ROWS, width), jnp.float32),
            in_specs=[HBM] * (4 + len(arrays) + len(adds)),
            out_specs=VMEM,
            scratch_shapes=[
                pltpu.VMEM((ROWS, n * BS), jnp.bfloat16),
                pltpu.VMEM((n, BS, width), jnp.bfloat16),
                pltpu.VMEM((max(1, len(adds)), ROWS, width), jnp.float32),
                pltpu.SemaphoreType.DMA((2 + max(1, len(adds)),)),
            ],
            compiler_params=PARAMS,
            cost_estimate=pl.CostEstimate(
                flops=2 * ROWS * n * BS * width, bytes_accessed=2 * 2**20, transcendentals=0
            ),
        )(*b_all, *arrays, *adds)

    near_by = [
        (i * CORES + c, (i + (1, -1)[c]) % chips * CORES + c) for i in range(chips) for c in range(CORES)
    ]
    b_eff = b_turned = None
    b_all = [None] * 4
    turned = []
    for step in range(1, last + 1):
        for j in range(2):
            if (step, j) == (last, 1):
                continue
            sent = held[j][-1]
            if (step, j) == (5, 0):
                sent = after(sent, b_all[1])
            if j == 1 and step > 3:
                sent = after(sent, turned[step - 4])
            with jax.named_scope(f"stream_{j}_step_{step}"):
                held[j].append(lax.ppermute(sent, ("core", "col"), ring))
            if (step, j) == (1, 0):
                sizes_k = after(inner_sizes, held[1][0])
                b_eff = mask_call(
                    mask_b_kernel, b_panel.shape[1:], mask_b, sizes_k, col_sizes, b_panel
                )
            if (step, j) == (1, 1):
                with jax.named_scope("b_swap"):
                    b_turned = lax.ppermute(b_eff, "core", SWAP)
            if (step, j) == (2, 1):
                b_all[0] = jnp.concatenate([b_eff, b_turned])
                with jax.named_scope("b_near"):
                    b_all[1] = lax.ppermute(b_all[0], ("y", "core"), near_by)
            if (step, j) == (3, 1):
                with jax.named_scope("b_far"):
                    b_all[3] = lax.ppermute(b_all[1], ("y", "core"), near_by)
            if (step, j) == (4, 1):
                with jax.named_scope("b_turn"):
                    b_all[2] = lax.ppermute(after(b_all[1], sent), "core", SWAP)
            if j == 1 and step > 1:
                turned.append(lax.ppermute(held[1][step - 1], "core", SWAP))
    turned.append(lax.ppermute(held[1][last - 1], "core", SWAP))

    shards = held[0] + turned[::-1]
    near = product(range(last - 1), shards[: last - 1])
    across = product(range(last + 2, cols), shards[last + 2 :])
    steps = range(last - 1, last + 2)
    parts = product(steps, [shards[s] for s in steps], (near, across), True)
    parts = parts.astype(jnp.float16)
    return decoded(lax.all_to_all(parts, "layer", 0, 0)).sum(axis=0)


def solution(mesh):
    rows, cols, layers = (mesh.shape[name] for name in ("row", "col", "layer"))
    devices = mesh.devices.reshape(rows // CORES, CORES, cols, layers)
    cores = Mesh(devices, ("y", "core", "col", "layer"))
    row = ("y", "core")
    return jax.shard_map(
        functools.partial(on_device, dict(cores.shape)),
        mesh=cores,
        in_specs=(
            P("layer", row, "col"),
            P("layer", row, "col"),
            P("layer", row, "col"),
            P("layer", row, "col"),
            P(row),
            P("layer", None),
            P("col"),
        ),
        out_specs=P((*row, "layer"), "col"),
        check_vma=False,
    )
```

```python
import functools

import jax
import jax.numpy as jnp
from jax import lax
from jax.experimental import pallas as pl
from jax.experimental.pallas import tpu as pltpu
from jax.sharding import Mesh, PartitionSpec as P

BS = 256
CORES = 2
ROWS = 1024
HBM = pl.BlockSpec(memory_space=pl.ANY)
VMEM = pl.BlockSpec(memory_space=pltpu.VMEM)
PARAMS = pltpu.CompilerParams(vmem_limit_bytes=40 * 1024 * 1024)
SWAP = [(0, 1), (1, 0)]
STEP, CODES, CODE_ROWS = 12, 10, 16


def below(axis, size):
    return lax.broadcasted_iota(jnp.int32, (BS, BS), axis) < size


def masked(block, rows, columns):
    kept = jnp.where(below(0, rows) & below(1, columns), block.astype(jnp.float32), 0.0)
    return kept.astype(jnp.bfloat16)


def fetched(refs):
    sems, refs = refs[-1], refs[:-1]
    count = len(refs) // 2
    copies = [pltpu.make_async_copy(refs[i], refs[count + 1 + i], sems.at[i]) for i in range(count)]
    for copy in copies:
        copy.start()
    for copy in copies:
        copy.wait()
    return refs[count], refs[count + 1 :]


def mask_a_kernel(*refs):
    out_ref, (mask, rows, inner, a) = fetched(refs)
    columns = inner[0, lax.axis_index("col")]
    for i in range(ROWS // BS):
        place = slice(i * BS, (i + 1) * BS)
        out_ref[place, :] = masked(a[0, place, :], rows[i] * mask[i], columns)


def mask_b_kernel(*refs):
    out_ref, (mask, inner, cols, b) = fetched(refs)
    first = (lax.axis_index("y") * CORES + lax.axis_index("core")) * mask.shape[1]
    for k in range(mask.shape[1]):
        for n in range(mask.shape[2]):
            place = (slice(k * BS, (k + 1) * BS), slice(n * BS, (n + 1) * BS))
            size = inner[0, first + k] * mask[0, k, n]
            out_ref[place] = masked(b[(0,) + place], size, cols[n])


def mask_call(kernel, shape, *args):
    spaces = [pltpu.SMEM] * (len(args) - 1) + [pltpu.VMEM]
    return pl.pallas_call(
        kernel,
        out_shape=jax.ShapeDtypeStruct(shape, jnp.bfloat16),
        in_specs=[pl.BlockSpec(memory_space=pltpu.HBM)] * len(args),
        out_specs=VMEM,
        scratch_shapes=[s(x.shape, x.dtype) for s, x in zip(spaces, args)]
        + [pltpu.SemaphoreType.DMA((len(args),))],
        compiler_params=pltpu.CompilerParams(vmem_limit_bytes=60 * 1024 * 1024),
    )(*args)


def product_kernel(steps, blocks, added, *refs):
    b_refs, refs = refs[:4], refs[4:]
    a_refs, refs = refs[: len(steps)], refs[len(steps) :]
    adds, (out_ref, a_all, b_all, extra, sems) = refs[:added], refs[added:]
    z, y, core = lax.axis_index("col"), lax.axis_index("y"), lax.axis_index("core")
    way = 2 * core - 1
    first, count = steps[0], len(steps)

    chips, mine, theirs = 4, core, 1 - core
    parts = (
        (0, 0, y, mine), (0, 1, y, theirs),
        (1, 0, y + way, mine), (1, 1, y + way, theirs),
        (2, 0, y - way, theirs), (2, 1, y - way, mine),
        (3, 0, y + 2, mine), (3, 1, y + 2, theirs),
    )
    for i, at, chip, owner in parts:
        for half in range(2):
            k = (lax.rem(chip + chips, chips) * CORES + owner) * 2 + half
            step = lax.rem(way * (k - z) + blocks, blocks)

            @pl.when((step >= first) & (step < first + count))
            def _(ref=b_refs[i], start=(at * 2 + half) * BS, step=step):
                pltpu.make_async_copy(
                    ref.at[pl.ds(start, BS)], b_all.at[step - first], sems.at[0]
                ).start()

    for i, ref in enumerate(a_refs):
        pltpu.make_async_copy(ref, a_all.at[:, pl.ds(i * BS, BS)], sems.at[1]).start()
    for i, ref in enumerate(adds):
        pltpu.make_async_copy(ref, extra.at[i], sems.at[2 + i]).start()
    pltpu.make_async_copy(b_all, b_all, sems.at[0]).wait()
    pltpu.make_async_copy(a_all, a_all, sems.at[1]).wait()
    for i, ref in enumerate(adds):
        pltpu.make_async_copy(ref, extra.at[i], sems.at[2 + i]).wait()

    b = b_all[...].reshape(count * BS, b_all.shape[2])
    for tile in range(ROWS // BS):
        rows = pl.ds(tile * BS, BS)
        total = jnp.dot(a_all[rows, :], b, preferred_element_type=jnp.float32)
        for i in range(added):
            total = total + extra[i, rows, :]
        if len(out_ref.shape) == 2:
            out_ref[rows, :] = total
        else:
            owners = out_ref.shape[0]
            encode(total, out_ref.at[lax.rem(tile - lax.axis_index("layer") + owners, owners)])


def encode(total, out_ref):
    top = jnp.max(jnp.abs(total), keepdims=True)
    scale, code = jnp.ones_like(top), jnp.zeros_like(top)
    for c in range(1, CODES + 1):
        small = top < 2.0 ** (14 - STEP * c)
        scale = jnp.where(small, 2.0 ** (STEP * c), scale)
        code = jnp.where(small, float(c), code)
    out_ref[:BS, :] = total * scale
    out_ref[BS:, :] = jnp.broadcast_to(code, (CODE_ROWS, total.shape[1]))


def decoded(parts):
    code = parts[:, BS:, :1].astype(jnp.float32).max(axis=1, keepdims=True)
    scale = jnp.ones_like(code)
    for c in range(1, CODES + 1):
        scale = jnp.where(code > c - 0.5, 2.0 ** (-STEP * c), scale)
    return parts[:, :BS].astype(jnp.float32) * scale


def after(value, earlier):
    return lax.optimization_barrier((value, earlier))[0]


def on_device(sizes, a_panel, b_panel, mask_a, mask_b, row_sizes, inner_sizes, col_sizes):
    cols, chips = sizes["col"], sizes["y"]
    width = b_panel.shape[2]
    ring = [
        (c * cols + i, c * cols + (i + (1, -1)[c]) % cols) for c in range(CORES) for i in range(cols)
    ]
    own = mask_call(
        mask_a_kernel, a_panel.shape[1:], mask_a.reshape(-1), row_sizes, inner_sizes, a_panel
    )

    last = cols // 2
    held = [[own], [lax.ppermute(own, "core", SWAP)]]

    def product(steps, arrays, adds=(), coded=False):
        n = len(steps)
        return pl.pallas_call(
            functools.partial(product_kernel, steps, cols, len(adds)),
            out_shape=jax.ShapeDtypeStruct((ROWS // BS, BS + CODE_ROWS, width), jnp.float32)
            if coded
            else jax.ShapeDtypeStruct((ROWS, width), jnp.float32),
            in_specs=[HBM] * (4 + len(arrays) + len(adds)),
            out_specs=VMEM,
            scratch_shapes=[
                pltpu.VMEM((ROWS, n * BS), jnp.bfloat16),
                pltpu.VMEM((n, BS, width), jnp.bfloat16),
                pltpu.VMEM((max(1, len(adds)), ROWS, width), jnp.float32),
                pltpu.SemaphoreType.DMA((2 + max(1, len(adds)),)),
            ],
            compiler_params=PARAMS,
            cost_estimate=pl.CostEstimate(
                flops=2 * ROWS * n * BS * width, bytes_accessed=2 * 2**20, transcendentals=0
            ),
        )(*b_all, *arrays, *adds)

    near_by = [
        (i * CORES + c, (i + (1, -1)[c]) % chips * CORES + c) for i in range(chips) for c in range(CORES)
    ]
    b_eff = b_turned = None
    b_all = [None] * 4
    turned = []
    for step in range(1, last + 1):
        for j in range(2):
            if (step, j) == (last, 1):
                continue
            sent = held[j][-1]
            if (step, j) == (5, 0):
                sent = after(sent, b_all[1])
            if j == 1 and step > 3:
                sent = after(sent, turned[step - 4])
            with jax.named_scope(f"stream_{j}_step_{step}"):
                held[j].append(lax.ppermute(sent, ("core", "col"), ring))
            if (step, j) == (1, 0):
                sizes_k = after(inner_sizes, held[1][0])
                b_eff = mask_call(
                    mask_b_kernel, b_panel.shape[1:], mask_b, sizes_k, col_sizes, b_panel
                )
            if (step, j) == (1, 1):
                with jax.named_scope("b_swap"):
                    b_turned = lax.ppermute(b_eff, "core", SWAP)
            if (step, j) == (2, 1):
                b_all[0] = jnp.concatenate([b_eff, b_turned])
                with jax.named_scope("b_near"):
                    b_all[1] = lax.ppermute(b_all[0], ("y", "core"), near_by)
            if (step, j) == (3, 1):
                with jax.named_scope("b_far"):
                    b_all[3] = lax.ppermute(b_all[1], ("y", "core"), near_by)
            if (step, j) == (4, 1):
                with jax.named_scope("b_turn"):
                    b_all[2] = lax.ppermute(after(b_all[1], sent), "core", SWAP)
            if j == 1 and step > 1:
                turned.append(lax.ppermute(held[1][step - 1], "core", SWAP))
    turned.append(lax.ppermute(held[1][last - 1], "core", SWAP))

    shards = held[0] + turned[::-1]
    near = product(range(last - 1), shards[: last - 1])
    across = product(range(last + 2, cols), shards[last + 2 :])
    steps = range(last - 1, last + 2)
    parts = product(steps, [shards[s] for s in steps], (near, across), True)
    layers = sizes["layer"]
    total = decoded(parts[:1])[0]
    for d in (2, 1, 3):
        pairs = [(i, (i + d) % layers) for i in range(layers)]
        part = lax.ppermute(parts[d : d + 1].astype(jnp.float16), "layer", pairs)
        total = total + decoded(part)[0]
    return total


def solution(mesh):
    rows, cols, layers = (mesh.shape[name] for name in ("row", "col", "layer"))
    devices = mesh.devices.reshape(rows // CORES, CORES, cols, layers)
    cores = Mesh(devices, ("y", "core", "col", "layer"))
    row = ("y", "core")
    return jax.shard_map(
        functools.partial(on_device, dict(cores.shape)),
        mesh=cores,
        in_specs=(
            P("layer", row, "col"),
            P("layer", row, "col"),
            P("layer", row, "col"),
            P("layer", row, "col"),
            P(row),
            P("layer", None),
            P("col"),
        ),
        out_specs=P((*row, "layer"), "col"),
        check_vma=False,
    )
```
